256 devices in a mesh: dp: 4 (over z_hi), ctx: 64 (over z_lo, y, x, core).
Axes of the slice: x: 4, y: 4, z: 8 (z_hi: 4, z_lo: 2; z = z_hi * 2 + z_lo), core: 2. Of those that a mesh axis runs over, the one named last changes fastest.
Arguments:
- queries: bfloat16 [4, 16384, 2560], P('dp', 'ctx'), may hold values from -120 to 120
- key_rows: bfloat16 [4, 16384, 512], P('dp', 'ctx'), may hold values from -6 to 6
- value_rows: bfloat16 [4, 16384, 512], P('dp', 'ctx'), may hold values from -6 to 6
- grad_out: bfloat16 [4, 16384, 2560], P('dp', 'ctx'), may hold values from -6 to 6
- doc_lengths: int32 [4, 32], P('dp'), may hold values from 1 to 1024, 16384 in all within a row
Outputs:
- attn_out: bfloat16 [4, 16384, 2560], P('dp', 'ctx')
- grad_queries: bfloat16 [4, 16384, 2560], P('dp', 'ctx')
- grad_keys: bfloat16 [4, 16384, 512], P('dp', 'ctx')
- grad_values: bfloat16 [4, 16384, 512], P('dp', 'ctx')
- bias_grad: float32 [3584], replicated
The draws below stay inside these ranges and needn't reach their ends.
Inputs may be any that keep to these rules, and one draw needn't show every extreme that they name: `doc_lengths`: each row's 32 lengths sum to 16384, and the largest in each row is exactly 1024.
All inputs are finite; a program needn't handle non-finite values.
Results may differ from the reference program's by a relative error of at most 0.012.
The reference program's roundings to bfloat16 on the way (of `probs_low` and `dscores`) count: a program that leaves them out, or rounds other values in their place, can miss the bound.
Values may be sent and summed in bfloat16 or wider, within the bound.
A program may use at most 128 MiB of HBM per device.

```python
import math
import jax
import jax.numpy as jnp
import numpy as np
from jax import lax

QH = 20
KVH = 4
HD = 128
GROUP = 5
TOK_DEV = 256
DOC_SPAN = 4
DOC_MAX = 1024
ROWS = 4
TOKENS = 16384
DOCS = 32
N_CTX = 64


def key_law(key):
    raw = jnp.clip(jax.random.normal(jax.random.fold_in(key, 11), (ROWS, TOKENS, KVH * HD), jnp.float32), -5.0, 5.0)
    return raw


def draw_key_rows(key, part):
    shared = key_law(key)
    return shared.astype(jnp.bfloat16)


def draw_queries(key, part):
    key = jax.random.fold_in(key, 5)
    base = jnp.clip(jax.random.normal(key, (ROWS, TOKENS, QH * HD), jnp.float32), -5.5, 5.5)
    return base.astype(jnp.bfloat16)


def levels(stream_key, extent, cuts, low, top_value):
    def one(axis_at, shards_of):
        heights = jax.random.uniform(jax.random.fold_in(jax.random.fold_in(stream_key, 6), axis_at), (shards_of,), jnp.float32, low / len(cuts), top_value / len(cuts))
        return jnp.repeat(jnp.exp(heights), extent[axis_at] // shards_of).reshape((-1,) + (1,) * (len(extent) - axis_at - 1))

    level = one(*cuts[0])
    for cut in cuts[1:]:
        level = level * one(*cut)
    return level


def length_profile(count, total, most, lean):
    weights = [(1 << 20) // math.isqrt(standing ** lean) + 1 for standing in range(2, count + 1)]
    spare, holding = total - most - (count - 1), [1] * (count - 1)
    while spare > 0:
        candidates = [i for i in range(count - 1) if holding[i] < most]
        mass, left = sum([weights[i] for i in candidates]), spare
        for i in candidates:
            more = min(most - holding[i], max(1, left * weights[i] // mass), spare)
            holding[i] = holding[i] + more
            spare = spare - more
    return np.array([most] + holding)


def uneven(stream_key, amount, total, most, lean):
    if amount == 2:
        one = jax.random.randint(stream_key, (), max(1, total - most), min(most, total - 1) + 1)
        return jnp.stack([one, total - one])
    sizes = jnp.asarray(length_profile(amount, total, most, lean), jnp.int32)
    couples = (amount - 1) // 2
    giver, taker = sizes[1:1 + 2 * couples:2], sizes[2:2 + 2 * couples:2]
    room = jnp.minimum(giver - 1, most - taker)
    shifted = jax.random.randint(jax.random.fold_in(stream_key, 1), (couples,), 0, 1 << 20) % (room + 1)
    sizes = sizes.at[1:1 + 2 * couples:2].set(giver - shifted).at[2:2 + 2 * couples:2].set(taker + shifted)
    return sizes[jax.random.permutation(jax.random.fold_in(stream_key, 2), amount)]


def centred(key, extent, deviation, limit, pieces=(), kind=jnp.bfloat16):
    factor_of = levels(key, extent, pieces, -0.22, 0.18) if pieces else 1.0
    drawn = jax.random.normal(key, extent, jnp.float32) * deviation * factor_of
    return jnp.minimum(jnp.maximum(drawn, -limit), limit).astype(kind)


def setup_inputs(seed: int = 0) -> dict:
    seeds = jax.random.split(jax.random.key(seed), 6)
    queries = draw_queries(jax.random.fold_in(seeds[5], 71), 0)
    key_rows = draw_key_rows(jax.random.fold_in(seeds[5], 71), 0)
    value_rows = centred(seeds[2], (ROWS, TOKENS, KVH * HD), 1.0, 6.0, ((0, 4), (1, 64)))
    grad_out = centred(seeds[3], (ROWS, TOKENS, QH * HD), 1.0, 6.0, ((0, 4), (1, 64)))
    doc_lengths = jax.vmap(lambda own: uneven(own, DOCS, TOKENS, DOC_MAX, 2))(jax.random.split(seeds[4], ROWS)).reshape((ROWS, DOCS)).astype(jnp.int32)
    return {"queries": queries, "key_rows": key_rows, "value_rows": value_rows, "grad_out": grad_out, "doc_lengths": doc_lengths}


def positions_doc(positions, bounds):
    return lax.optimization_barrier(jnp.sum((positions[:, None] >= bounds[None, :]).astype(jnp.int32), axis=1))

def window_attention(query_block, key_window, value_window, grad_block, query_pos, key_pos, bounds):
    rows_query = query_block.shape[0]
    rows_key = key_window.shape[0]
    query_doc = positions_doc(query_pos, bounds)
    key_doc = positions_doc(key_pos, bounds)
    allowed = (query_doc[:, None] == key_doc[None, :]) & (key_pos[None, :] <= query_pos[:, None]) & (key_pos[None, :] >= 0)
    scale = 1.0 / math.sqrt(HD)
    grouped_query = query_block.reshape(rows_query, KVH, GROUP, HD).transpose(1, 2, 0, 3)
    grouped_grad = grad_block.reshape(rows_query, KVH, GROUP, HD).transpose(1, 2, 0, 3)
    keyed = key_window.reshape(rows_key, KVH, HD).transpose(1, 0, 2)
    valued = value_window.reshape(rows_key, KVH, HD).transpose(1, 0, 2)

    def per_head(operands):
        query_head, key_head, value_head, grad_head = operands
        scores = jnp.einsum('gtd,sd->gts', query_head, key_head, preferred_element_type=jnp.float32) * scale
        masked = jnp.where(allowed[None], scores, jnp.float32(-1e+30))
        top_score = lax.optimization_barrier(jnp.max(masked, axis=-1, keepdims=True))
        weights = jnp.where(allowed[None], jnp.exp(masked - top_score), jnp.float32(0.0))
        probs = weights / lax.optimization_barrier(jnp.sum(weights, axis=-1, keepdims=True))
        probs_low = probs.astype(jnp.bfloat16)
        attn = jnp.einsum('gts,sd->gtd', probs_low, value_head, preferred_element_type=jnp.float32).astype(jnp.bfloat16)
        dprobs = jnp.einsum('gtd,sd->gts', grad_head, value_head, preferred_element_type=jnp.float32)
        delta = lax.optimization_barrier(jnp.sum(grad_head.astype(jnp.float32) * attn.astype(jnp.float32), axis=-1, keepdims=True))
        dscores = (probs * (dprobs - delta) * scale).astype(jnp.bfloat16)
        dquery = jnp.einsum('gts,sd->gtd', dscores, key_head, preferred_element_type=jnp.float32)
        dkey = jnp.einsum('gts,gtd->sd', dscores, query_head, preferred_element_type=jnp.float32)
        dvalue = jnp.einsum('gts,gtd->sd', probs_low, grad_head, preferred_element_type=jnp.float32)
        return (attn, dquery, dkey, dvalue)
    attn, dquery, dkey, dvalue = lax.map(per_head, (grouped_query, keyed, valued, grouped_grad))
    attn = attn.transpose(2, 0, 1, 3).reshape(rows_query, KVH * GROUP * HD)
    dquery = dquery.transpose(2, 0, 1, 3).reshape(rows_query, KVH * GROUP * HD)
    dkey = dkey.transpose(1, 0, 2).reshape(rows_key, KVH * HD)
    dvalue = dvalue.transpose(1, 0, 2).reshape(rows_key, KVH * HD)
    return (attn, dquery, dkey, dvalue)

def one_row(query_row, key_row, value_row, grad_row, lengths):
    bounds = jnp.cumsum(lengths).astype(jnp.int32)
    margin = DOC_SPAN * TOK_DEV
    window = (DOC_SPAN + 1) * TOK_DEV
    kv_width = key_row.shape[1]
    key_pad = jnp.concatenate([jnp.zeros((margin, kv_width), jnp.bfloat16), key_row], axis=0)
    value_pad = jnp.concatenate([jnp.zeros((margin, kv_width), jnp.bfloat16), value_row], axis=0)

    def step(carry, block):
        key_acc, value_acc = carry
        start = (block * TOK_DEV).astype(jnp.int32)
        query_block = lax.dynamic_slice_in_dim(query_row, start, TOK_DEV, 0)
        grad_block = lax.dynamic_slice_in_dim(grad_row, start, TOK_DEV, 0)
        key_window = lax.dynamic_slice_in_dim(key_pad, start, window, 0)
        value_window = lax.dynamic_slice_in_dim(value_pad, start, window, 0)
        query_pos = start + jnp.arange(TOK_DEV, dtype=jnp.int32)
        key_pos = start - margin + jnp.arange(window, dtype=jnp.int32)
        attn, dquery, dkey, dvalue = window_attention(query_block, key_window, value_window, grad_block, query_pos, key_pos, bounds)
        key_acc = lax.dynamic_update_slice_in_dim(key_acc, lax.dynamic_slice_in_dim(key_acc, start, window, 0) + dkey, start, 0)
        value_acc = lax.dynamic_update_slice_in_dim(value_acc, lax.dynamic_slice_in_dim(value_acc, start, window, 0) + dvalue, start, 0)
        return ((key_acc, value_acc), (attn, dquery.astype(jnp.bfloat16), lax.optimization_barrier(jnp.sum(dquery, axis=0))))
    zeros = jnp.zeros((margin + TOKENS, kv_width), jnp.float32)
    (key_acc, value_acc), (attn, dquery, dquery_sums) = lax.scan(step, (zeros, zeros), jnp.arange(N_CTX, dtype=jnp.int32))
    dkey_full = key_acc[margin:]
    dvalue_full = value_acc[margin:]
    sums = jnp.concatenate([lax.optimization_barrier(jnp.sum(dquery_sums, axis=0)), lax.optimization_barrier(jnp.sum(dkey_full, axis=0)), lax.optimization_barrier(jnp.sum(dvalue_full, axis=0))])
    return (attn.reshape(TOKENS, -1), dquery.reshape(TOKENS, -1), dkey_full.astype(jnp.bfloat16), dvalue_full.astype(jnp.bfloat16), sums)

def reference(queries, key_rows, value_rows, grad_out, doc_lengths):
    outputs = [one_row(queries[row], key_rows[row], value_rows[row], grad_out[row], doc_lengths[row]) for row in range(ROWS)]
    attn_out = jnp.stack([item[0] for item in outputs])
    grad_queries = jnp.stack([item[1] for item in outputs])
    grad_keys = jnp.stack([item[2] for item in outputs])
    grad_values = jnp.stack([item[3] for item in outputs])
    bias_grad = outputs[0][4]
    for item in outputs[1:]:
        bias_grad = bias_grad + item[4]
    return (attn_out, grad_queries, grad_keys, grad_values, bias_grad)
```

```python
import math

import jax
import jax.numpy as jnp
from jax import lax
from jax.experimental import pallas as pl
from jax.experimental.pallas import tpu as pltpu
from jax.sharding import PartitionSpec as P

KVH = 4
HD = 128
GROUP = 5
TOK = 256
SPAN = 4
WIN = (SPAN + 1) * TOK
HALF = 128
HWIN = SPAN * TOK + HALF
GW = GROUP * HD
DOCS = 32
SCALE = 1.0 / math.sqrt(HD)
SCALE2 = SCALE * math.log2(math.e)
NT = (((1,), (1,)), ((), ()))
MESH = pl.DeviceIdType.MESH
F32 = jnp.float32
BF16 = jnp.bfloat16
COMPUTE = True


def kernel(
    lens, q_hbm, k_hbm, v_hbm, do_hbm,
    o_hbm, dq_hbm, dk_hbm, dv_hbm, bias_out,
    q, do, ob, dqb, kv, part, stage, got, okv, mask, dkt, dvt,
    sums, b1, b2, b3,
    load_sem, kv_sem, out_sem, okv_sem,
    fs, fr, rs, rr, bs, br1, br2, br3,
):
    dp = lax.axis_index("dp")
    me = lax.axis_index("ctx")
    n = 64
    core = lax.rem(me, 2)
    nxt = lax.rem(me + 2, n)
    prv = lax.rem(me + n - 2, n)
    mate = me + 1 - 2 * core
    rank1 = lax.rem(me, 8)
    rank2 = lax.rem(me // 8, 4)
    zlo = me // 32
    rank3 = dp * 2 + zlo

    def peer1(d):
        return (dp, me - rank1 + lax.rem(rank1 + d, 8))

    def peer2(d):
        return (dp, me + 8 * (lax.rem(rank2 + d, 4) - rank2))

    def peer3(d):
        r = lax.rem(rank3 + d, 8)
        return (r // 2, me + 32 * (lax.rem(r, 2) - zlo))

    def kvload(g):
        c = g * HD
        return (
            pltpu.make_async_copy(k_hbm.at[0, :, pl.ds(c, HD)], kv.at[g, 0, pl.ds(SPAN * TOK, TOK)], kv_sem.at[g, 0]),
            pltpu.make_async_copy(v_hbm.at[0, :, pl.ds(c, HD)], kv.at[g, 1, pl.ds(SPAN * TOK, TOK)], kv_sem.at[g, 1]),
        )

    def qload(g):
        c = pl.ds(pl.multiple_of(g * GW, 128), GW)
        return (
            pltpu.make_async_copy(q_hbm.at[0, :, c], q.at[:, c], load_sem.at[g, 0]),
            pltpu.make_async_copy(do_hbm.at[0, :, c], do.at[:, c], load_sem.at[g, 1]),
        )

    def ostore(g):
        c = pl.ds(pl.multiple_of(g * GW, 128), GW)
        return (
            pltpu.make_async_copy(ob.at[:, c], o_hbm.at[0, :, c], out_sem.at[g, 0]),
            pltpu.make_async_copy(dqb.at[:, c], dq_hbm.at[0, :, c], out_sem.at[g, 1]),
        )

    def fwd(kind, g, src_slot, dst_slot, to):
        return pltpu.make_async_remote_copy(
            src_ref=kv.at[g, :, pl.ds(src_slot * TOK, TOK)],
            dst_ref=kv.at[g, :, pl.ds(dst_slot * TOK, TOK)],
            send_sem=fs.at[g, kind],
            recv_sem=fr.at[g, kind],
            device_id=(dp, to),
            device_id_type=MESH,
        )

    def h1(g):
        return fwd(0, g, 4, 2, nxt)

    def h2(g):
        return fwd(1, g, 2, 0, nxt)

    def l1(g):
        return fwd(2, g, 4, 3, mate)

    def l2_from0(g):
        return fwd(3, g, 2, 1, mate)

    def l2_from1(g):
        return fwd(3, g, 2, 3, mate)

    def l3(g):
        return fwd(4, g, 0, 1, mate)

    def relay1(g):
        h1(g).wait_recv()
        h2(g).start()

        @pl.when(core == 0)
        def _():
            l2_from0(g).start()

        @pl.when(core == 1)
        def _():
            l2_from1(g).start()

    def relay2(g):
        h2(g).wait_recv()

        @pl.when(core == 1)
        def _():
            l3(g).start()

    def complete(g):
        @pl.when(core == 0)
        def _():
            l2_from1(g).wait_recv()
            l3(g).wait_recv()

        @pl.when(core == 1)
        def _():
            l1(g).wait_recv()
            l2_from0(g).wait_recv()

    def begin(g):
        h1(g).start()

        @pl.when(core == 0)
        def _():
            l1(g).start()

    def ret(kind, g, to):
        return pltpu.make_async_remote_copy(
            src_ref=stage.at[g, kind],
            dst_ref=got.at[g, kind],
            send_sem=rs.at[g, kind],
            recv_sem=rr.at[g, kind],
            device_id=(dp, to),
            device_id_type=MESH,
        )

    def r1(g):
        for kind, slot in ((0, 1), (1, 3)):
            for t in range(2):
                stage[g, kind, t] = part[g, t, slot * TOK:(slot + 1) * TOK].astype(BF16)
            ret(kind, g, mate).start()

    def r2(g):
        ret(0, g, mate).wait_recv()

        @pl.when(core == 0)
        def _():
            for t in range(2):
                stage[g, 2, t] = part[g, t, 0:TOK].astype(BF16)

        @pl.when(core == 1)
        def _():
            for t in range(2):
                stage[g, 2, t] = (part[g, t, 0:TOK] + got[g, 0, t].astype(F32)).astype(BF16)

        ret(2, g, prv).start()

    def r3(g):
        ret(1, g, mate).wait_recv()
        ret(2, g, prv).wait_recv()
        mine = slice(2 * TOK, 3 * TOK)

        @pl.when(core == 0)
        def _():
            for t in range(2):
                stage[g, 3, t] = (part[g, t, mine] + got[g, 0, t].astype(F32) + got[g, 2, t].astype(F32)).astype(BF16)

        @pl.when(core == 1)
        def _():
            for t in range(2):
                stage[g, 3, t] = (part[g, t, mine] + got[g, 1, t].astype(F32) + got[g, 2, t].astype(F32)).astype(BF16)

        ret(3, g, prv).start()

    def okv_store(g):
        c = pl.ds(pl.multiple_of(g * HD, 128), HD)
        return (
            pltpu.make_async_copy(okv.at[g, 0], dk_hbm.at[0, :, c], okv_sem.at[g, 0]),
            pltpu.make_async_copy(okv.at[g, 1], dv_hbm.at[0, :, c], okv_sem.at[g, 1]),
        )

    def r4(g):
        ret(3, g, prv).wait_recv()
        mine = slice(4 * TOK, 5 * TOK)

        @pl.when(core == 0)
        def _():
            for t in range(2):
                okv[g, t] = (part[g, t, mine] + got[g, 1, t].astype(F32) + got[g, 3, t].astype(F32)).astype(BF16)

        @pl.when(core == 1)
        def _():
            for t in range(2):
                okv[g, t] = (part[g, t, mine] + got[g, 3, t].astype(F32)).astype(BF16)

        for c in okv_store(g):
            c.start()

    def bias_send(buf, rank, peer, size, sem_at, recv):
        for d in range(1, size):
            pltpu.make_async_remote_copy(
                src_ref=buf.at[rank],
                dst_ref=buf.at[rank],
                send_sem=bs.at[sem_at + d],
                recv_sem=recv.at[rank],
                device_id=peer(d),
                device_id_type=MESH,
            ).start()

    def bias_wait(buf, rank, peer, size, sem_at, recv):
        for d in range(1, size):
            other = lax.rem(rank + d, size)
            pltpu.make_async_remote_copy(
                src_ref=buf.at[rank],
                dst_ref=buf.at[other],
                send_sem=bs.at[sem_at + d],
                recv_sem=recv.at[other],
                device_id=peer(d),
                device_id_type=MESH,
            ).wait()
        total = buf[0]
        for r in range(1, size):
            total = total + buf[r]
        return total

    for g in range(KVH):
        for c in kvload(g):
            c.start()
    for g in range(KVH):
        for c in qload(g):
            c.start()

    barrier = pltpu.get_barrier_semaphore()
    peers = [(dp, nxt), (dp, prv)]
    peers += [peer1(d) for d in range(1, 8)]
    peers += [peer2(d) for d in range(1, 4)]
    peers += [peer3(d) for d in range(1, 8)]
    for p in peers:
        pl.semaphore_signal(barrier, inc=1, device_id=p, device_id_type=MESH)
    pl.semaphore_wait(barrier, len(peers))

    for g in range(2):
        for c in kvload(g):
            c.wait()
        begin(g)

    where = me * TOK
    t_pos = lax.broadcasted_iota(jnp.int32, (TOK, 128), 0) + where
    first = jnp.zeros((TOK, 128), jnp.int32)
    bound = jnp.int32(0)
    for i in range(DOCS):
        bound = bound + lens[0, i]
        first = jnp.where(t_pos >= bound, bound, first)
    for c in range(WIN // 128):
        s_pos = lax.broadcasted_iota(jnp.int32, (TOK, 128), 1) + (where - SPAN * TOK + c * 128)
        mask[:, c * 128:(c + 1) * 128] = jnp.where((s_pos >= first) & (s_pos <= t_pos), 0.0, -1e30).astype(F32)

    for c in kvload(2):
        c.wait()
    relay1(0)
    begin(2)
    for c in kvload(3):
        c.wait()
    relay1(1)
    relay2(0)

    def unit(g, h):
        w0 = h * HALF
        rows = slice(w0, w0 + HALF)
        K = kv[g, 0, w0:w0 + HWIN]
        V = kv[g, 1, w0:w0 + HWIN]
        cols = [pl.ds(pl.multiple_of(g * GW + j * HD, 128), HD) for j in range(GROUP)]
        Q = jnp.concatenate([q[rows, c] for c in cols], 0)
        D = jnp.concatenate([do[rows, c] for c in cols], 0)
        bias = jnp.concatenate([mask[rows, w0:w0 + HWIN]] * GROUP, 0)
        s = lax.dot_general(Q, K, NT, preferred_element_type=F32) * SCALE2 + bias
        dprobs = lax.dot_general(D, V, NT, preferred_element_type=F32)
        m = jnp.max(s, axis=1, keepdims=True)
        w = jnp.exp2(s - m)
        inv = 1.0 / jnp.sum(w, axis=1, keepdims=True)
        low = (w * inv).astype(BF16)
        o = jnp.dot(low, V, preferred_element_type=F32).astype(BF16)
        delta = jnp.sum(D.astype(F32) * o.astype(F32), axis=1, keepdims=True)
        ds = ((w * (inv * SCALE)) * (dprobs - delta)).astype(BF16)
        dq = jnp.dot(ds, K, preferred_element_type=F32)
        for j, c in enumerate(cols):
            ob[rows, c] = o[j * HALF:(j + 1) * HALF]
            dqj = dq[j * HALF:(j + 1) * HALF]
            dqb[rows, c] = dqj.astype(BF16)
            dqs = jnp.sum(dqj, axis=0, keepdims=True)
            if h == 0:
                sums[g, j:j + 1] = dqs
            else:
                sums[g, j:j + 1] += dqs
        a1 = jnp.dot(Q.T, ds, preferred_element_type=F32)
        a2 = jnp.dot(D.T, low, preferred_element_type=F32)
        if h == 0:
            dkt[:, :HWIN] = a1
            dvt[:, :HWIN] = a2
            dkt[:, HWIN:] = jnp.zeros((HD, WIN - HWIN), F32)
            dvt[:, HWIN:] = jnp.zeros((HD, WIN - HWIN), F32)
        else:
            dkt[:, w0:] += a1
            dvt[:, w0:] += a2

    def finish(g):
        dk = dkt[...].T
        dv = dvt[...].T
        part[g, 0] = dk
        part[g, 1] = dv
        sums[g, 5:6] = jnp.sum(dk, axis=0, keepdims=True)
        sums[g, 6:7] = jnp.sum(dv, axis=0, keepdims=True)
        sums[g, 7:8] = jnp.zeros((1, HD), F32)

    def body(g, carry):
        complete(g)
        for c in qload(g):
            c.wait()
        if COMPUTE:
            unit(g, 0)

        @pl.when(g < 3)
        def _():
            relay2(g + 1)

        @pl.when(g < 2)
        def _():
            relay1(g + 2)

        @pl.when(g < 1)
        def _():
            begin(g + 3)

        @pl.when(g > 0)
        def _():
            r2(g - 1)

        @pl.when(g > 1)
        def _():
            r4(g - 2)

        if COMPUTE:
            unit(g, 1)
            finish(g)
        r1(g)
        for c in ostore(g):
            c.start()

        @pl.when(g > 0)
        def _():
            r3(g - 1)

        return carry

    lax.fori_loop(0, KVH, body, 0)

    b1[rank1] = sums[...]
    bias_send(b1, rank1, peer1, 8, 0, br1)
    r2(3)
    total = bias_wait(b1, rank1, peer1, 8, 0, br1)
    b2[rank2] = total
    bias_send(b2, rank2, peer2, 4, 8, br2)
    r4(2)
    r3(3)
    total = bias_wait(b2, rank2, peer2, 4, 8, br2)
    b3[rank3] = total
    bias_send(b3, rank3, peer3, 8, 12, br3)
    total = bias_wait(b3, rank3, peer3, 8, 12, br3)
    for g in range(KVH):
        bias_out[g * GROUP:(g + 1) * GROUP] = total[g, 0:GROUP]
        bias_out[20 + g:21 + g] = total[g, 5:6]
        bias_out[24 + g:25 + g] = total[g, 6:7]
    r4(3)

    def drain(g, carry):
        h1(g).wait_send()
        h2(g).wait_send()

        @pl.when(core == 0)
        def _():
            l1(g).wait_send()
            l2_from0(g).wait_send()

        @pl.when(core == 1)
        def _():
            l2_from1(g).wait_send()
            l3(g).wait_send()

        ret(0, g, mate).wait_send()
        ret(1, g, mate).wait_send()
        ret(2, g, prv).wait_send()
        ret(3, g, prv).wait_send()
        for c in ostore(g) + okv_store(g):
            c.wait()
        return carry

    lax.fori_loop(0, KVH, drain, 0)


def on_device(queries, key_rows, value_rows, grad_out, doc_lengths):
    hbm = pl.BlockSpec(memory_space=pl.ANY)
    dma = pltpu.SemaphoreType.DMA
    wide = jax.ShapeDtypeStruct((1, TOK, KVH * GW), BF16)
    narrow = jax.ShapeDtypeStruct((1, TOK, KVH * HD), BF16)
    o, dq, dk, dv, bias = pl.pallas_call(
        kernel,
        out_shape=(wide, wide, narrow, narrow, jax.ShapeDtypeStruct((28, HD), F32)),
        in_specs=[pl.BlockSpec(memory_space=pltpu.SMEM)] + [hbm] * 4,
        out_specs=[hbm] * 4 + [pl.BlockSpec(memory_space=pltpu.VMEM)],
        scratch_shapes=[
            pltpu.VMEM((TOK, KVH * GW), BF16),
            pltpu.VMEM((TOK, KVH * GW), BF16),
            pltpu.VMEM((TOK, KVH * GW), BF16),
            pltpu.VMEM((TOK, KVH * GW), BF16),
            pltpu.VMEM((KVH, 2, WIN, HD), BF16),
            pltpu.VMEM((KVH, 2, WIN, HD), F32),
            pltpu.VMEM((KVH, 4, 2, TOK, HD), BF16),
            pltpu.VMEM((KVH, 4, 2, TOK, HD), BF16),
            pltpu.VMEM((KVH, 2, TOK, HD), BF16),
            pltpu.VMEM((TOK, WIN), F32),
            pltpu.VMEM((HD, WIN), F32),
            pltpu.VMEM((HD, WIN), F32),
            pltpu.VMEM((KVH, 8, HD), F32),
            pltpu.VMEM((8, KVH, 8, HD), F32),
            pltpu.VMEM((4, KVH, 8, HD), F32),
            pltpu.VMEM((8, KVH, 8, HD), F32),
            dma((KVH, 2)),
            dma((KVH, 2)),
            dma((KVH, 2)),
            dma((KVH, 2)),
            dma((KVH, 5)),
            dma((KVH, 5)),
            dma((KVH, 4)),
            dma((KVH, 4)),
            dma((20,)),
            dma((8,)),
            dma((4,)),
            dma((8,)),
        ],
        compiler_params=pltpu.CompilerParams(
            collective_id=0, has_side_effects=True, vmem_limit_bytes=56 * 1024 * 1024
        ),
        cost_estimate=pl.CostEstimate(flops=10_000_000_000, bytes_accessed=8_000_000, transcendentals=6_000_000),
    )(doc_lengths, queries, key_rows, value_rows, grad_out)
    return o, dq, dk, dv, bias.reshape(28 * HD)


def solution(mesh):
    spec = P("dp", "ctx", None)
    return jax.shard_map(
        on_device,
        mesh=mesh,
        in_specs=(spec, spec, spec, spec, P("dp", None)),
        out_specs=(spec, spec, spec, spec, P()),
        check_vma=False,
    )
```

```python
import math

import jax
import jax.numpy as jnp
from jax import lax
from jax.experimental import pallas as pl
from jax.experimental.pallas import tpu as pltpu
from jax.sharding import PartitionSpec as P

KVH = 4
HD = 128
GROUP = 5
TOK = 256
SPAN = 4
WIN = (SPAN + 1) * TOK
HALF = 128
HWIN = SPAN * TOK + HALF
GW = GROUP * HD
DOCS = 32
SCALE = 1.0 / math.sqrt(HD)
SCALE2 = SCALE * math.log2(math.e)
NT = (((1,), (1,)), ((), ()))
MESH = pl.DeviceIdType.MESH
F32 = jnp.float32
BF16 = jnp.bfloat16


def kernel(
    lens, q_hbm, k_hbm, v_hbm, do_hbm,
    ob, dqb, dk_out, dv_out, bias_out,
    q, do, kv, part, stage, got, mask, dkt, dvt, wkeep, lowkeep, stat,
    sums, b1, b2, b3,
    load_sem, kv_sem,
    fs, fr, rs, rr, bs, br1, br2, br3,
):
    dp = lax.axis_index("dp")
    me = lax.axis_index("ctx")
    n = 64
    core = lax.rem(me, 2)
    nxt = lax.rem(me + 2, n)
    prv = lax.rem(me + n - 2, n)
    mate = me + 1 - 2 * core
    rank1 = lax.rem(me, 8)
    rank2 = lax.rem(me // 8, 4)
    zlo = me // 32
    rank3 = dp * 2 + zlo

    def peer1(d):
        return (dp, me - rank1 + lax.rem(rank1 + d, 8))

    def peer2(d):
        return (dp, me + 8 * (lax.rem(rank2 + d, 4) - rank2))

    def peer3(d):
        r = lax.rem(rank3 + d, 8)
        return (r // 2, me + 32 * (lax.rem(r, 2) - zlo))

    def kvload(g):
        c = g * HD
        return (
            pltpu.make_async_copy(k_hbm.at[0, :, pl.ds(c, HD)], kv.at[g, 0, pl.ds(SPAN * TOK, TOK)], kv_sem.at[g, 0]),
            pltpu.make_async_copy(v_hbm.at[0, :, pl.ds(c, HD)], kv.at[g, 1, pl.ds(SPAN * TOK, TOK)], kv_sem.at[g, 1]),
        )

    def qload(g):
        c = pl.ds(pl.multiple_of(g * GW, 128), GW)
        return (
            pltpu.make_async_copy(q_hbm.at[0, :, c], q.at[:, c], load_sem.at[g, 0]),
            pltpu.make_async_copy(do_hbm.at[0, :, c], do.at[:, c], load_sem.at[g, 1]),
        )

    def fwd(kind, g, t, src_slot, dst_slot, to):
        return pltpu.make_async_remote_copy(
            src_ref=kv.at[g, t, pl.ds(src_slot * TOK, TOK)],
            dst_ref=kv.at[g, t, pl.ds(dst_slot * TOK, TOK)],
            send_sem=fs.at[g, kind, t],
            recv_sem=fr.at[g, kind, t],
            device_id=(dp, to),
            device_id_type=MESH,
        )

    def h1(g, t):
        return fwd(0, g, t, 4, 2, nxt)

    def h2(g, t):
        return fwd(1, g, t, 2, 0, nxt)

    def l1(g, t):
        return fwd(2, g, t, 4, 3, mate)

    def l2_from0(g, t):
        return fwd(3, g, t, 2, 1, mate)

    def l2_from1(g, t):
        return fwd(3, g, t, 2, 3, mate)

    def l3(g, t):
        return fwd(4, g, t, 0, 1, mate)

    def near(g, t):
        h1(g, t).wait_recv()
        h2(g, t).start()

        @pl.when(core == 0)
        def _():
            l2_from0(g, t).start()

        @pl.when(core == 1)
        def _():
            l2_from1(g, t).start()

    def far(g, t):
        h2(g, t).wait_recv()

        @pl.when(core == 1)
        def _():
            l3(g, t).start()

    def complete(g):
        @pl.when(core == 0)
        def _():
            for t in range(2):
                l2_from1(g, t).wait_recv()
                l3(g, t).wait_recv()

        @pl.when(core == 1)
        def _():
            for t in range(2):
                l1(g, t).wait_recv()
                l2_from0(g, t).wait_recv()

    def mate_send(g):
        @pl.when(core == 0)
        def _():
            for t in range(2):
                l1(g, t).start()

    def ret(kind, g, t, to):
        return pltpu.make_async_remote_copy(
            src_ref=stage.at[g, kind, t],
            dst_ref=got.at[g, kind, t],
            send_sem=rs.at[g, kind, t],
            recv_sem=rr.at[g, kind, t],
            device_id=(dp, to),
            device_id_type=MESH,
        )

    def r1(g, t):
        for kind, slot in ((0, 1), (1, 3)):
            stage[g, kind, t] = part[g, t, slot * TOK:(slot + 1) * TOK].astype(BF16)
            ret(kind, g, t, mate).start()

    def r2(g, t):
        ret(0, g, t, mate).wait_recv()

        @pl.when(core == 0)
        def _():
            stage[g, 2, t] = part[g, t, 0:TOK].astype(BF16)

        @pl.when(core == 1)
        def _():
            stage[g, 2, t] = (part[g, t, 0:TOK] + got[g, 0, t].astype(F32)).astype(BF16)

        ret(2, g, t, prv).start()
        ret(1, g, t, mate).wait_recv()

        @pl.when(core == 0)
        def _():
            part[g, t, 2 * TOK:3 * TOK] += got[g, 0, t].astype(F32)
            part[g, t, 4 * TOK:] += got[g, 1, t].astype(F32)

        @pl.when(core == 1)
        def _():
            part[g, t, 2 * TOK:3 * TOK] += got[g, 1, t].astype(F32)

    def r3(g, t):
        ret(2, g, t, prv).wait_recv()
        stage[g, 3, t] = (part[g, t, 2 * TOK:3 * TOK] + got[g, 2, t].astype(F32)).astype(BF16)
        ret(3, g, t, prv).start()

    def r4(g, t):
        ret(3, g, t, prv).wait_recv()
        c = pl.ds(pl.multiple_of(g * HD, 128), HD)
        (dk_out, dv_out)[t][0, :, c] = (part[g, t, 4 * TOK:] + got[g, 3, t].astype(F32)).astype(BF16)

    def bias_send(buf, rank, peer, size, sem_at, recv):
        for d in range(1, size):
            pltpu.make_async_remote_copy(
                src_ref=buf.at[rank],
                dst_ref=buf.at[rank],
                send_sem=bs.at[sem_at + d],
                recv_sem=recv.at[rank],
                device_id=peer(d),
                device_id_type=MESH,
            ).start()

    def bias_wait(buf, rank, peer, size, sem_at, recv):
        for d in range(1, size):
            other = lax.rem(rank + d, size)
            pltpu.make_async_remote_copy(
                src_ref=buf.at[rank],
                dst_ref=buf.at[other],
                send_sem=bs.at[sem_at + d],
                recv_sem=recv.at[other],
                device_id=peer(d),
                device_id_type=MESH,
            ).wait()
        total = buf[0]
        for r in range(1, size):
            total = total + buf[r]
        return total

    for g in range(KVH):
        for c in kvload(g):
            c.start()
    for g in range(KVH):
        for c in qload(g):
            c.start()

    barrier = pltpu.get_barrier_semaphore()
    peers = [(dp, nxt), (dp, prv)]
    peers += [peer1(d) for d in range(1, 8)]
    peers += [peer2(d) for d in range(1, 4)]
    peers += [peer3(d) for d in range(1, 8)]
    for p in peers:
        pl.semaphore_signal(barrier, inc=1, device_id=p, device_id_type=MESH)
    pl.semaphore_wait(barrier, len(peers))

    for t in range(2):
        kvload(0)[t].wait()
        h1(0, t).start()
    mate_send(0)
    for g in range(1, KVH):
        for c in kvload(g):
            c.wait()
        mate_send(g)
    for t in range(2):
        h1(0, t).wait_send()
        h1(1, t).start()

    where = me * TOK
    t_pos = lax.broadcasted_iota(jnp.int32, (TOK, 128), 0) + where
    first = jnp.zeros((TOK, 128), jnp.int32)
    bound = jnp.int32(0)
    for i in range(DOCS):
        bound = bound + lens[0, i]
        first = jnp.where(t_pos >= bound, bound, first)
    for c in range(WIN // 128):
        s_pos = lax.broadcasted_iota(jnp.int32, (TOK, 128), 1) + (where - SPAN * TOK + c * 128)
        mask[:, c * 128:(c + 1) * 128] = jnp.where((s_pos >= first) & (s_pos <= t_pos), 0.0, -1e30).astype(F32)

    for t in range(2):
        near(0, t)
    for t in range(2):
        near(1, t)
    for t in range(2):
        far(0, t)
    for t in range(2):
        h1(2, t).start()

    def stacked(g, h, of):
        rows = slice(h * HALF, (h + 1) * HALF)
        return jnp.concatenate([of[rows, c] for c in columns(g)], 0)

    def columns(g):
        return [pl.ds(pl.multiple_of(g * GW + j * HD, 128), HD) for j in range(GROUP)]

    def unit_a(g, h):
        w0 = h * HALF
        rows = slice(w0, w0 + HALF)
        K = kv[g, 0, w0:w0 + HWIN]
        V = kv[g, 1, w0:w0 + HWIN]
        Q = stacked(g, h, q)
        D = stacked(g, h, do)
        bias = jnp.concatenate([mask[rows, w0:w0 + HWIN]] * GROUP, 0)
        s = lax.dot_general(Q, K, NT, preferred_element_type=F32) * SCALE2 + bias
        m = jnp.max(s, axis=1, keepdims=True)
        w = jnp.exp2(s - m)
        inv = 1.0 / jnp.sum(w, axis=1, keepdims=True)
        low = (w * inv).astype(BF16)
        o = jnp.dot(low, V, preferred_element_type=F32).astype(BF16)
        delta = jnp.sum(D.astype(F32) * o.astype(F32), axis=1, keepdims=True)
        for j, c in enumerate(columns(g)):
            ob[0, rows, c] = o[j * HALF:(j + 1) * HALF]
        wkeep[...] = w
        lowkeep[...] = low
        stat[:, 0:128] = jnp.broadcast_to(inv * SCALE, (GROUP * HALF, 128))
        stat[:, 128:256] = jnp.broadcast_to(delta, (GROUP * HALF, 128))

    def unit_b(g, h):
        w0 = h * HALF
        rows = slice(w0, w0 + HALF)
        K = kv[g, 0, w0:w0 + HWIN]
        V = kv[g, 1, w0:w0 + HWIN]
        Q = stacked(g, h, q)
        D = stacked(g, h, do)
        dprobs = lax.dot_general(D, V, NT, preferred_element_type=F32)
        a2 = jnp.dot(D.T, lowkeep[...], preferred_element_type=F32)
        if h == 0:
            dvt[:, :HWIN] = a2
            dvt[:, HWIN:] = jnp.zeros((HD, WIN - HWIN), F32)
        else:
            dvt[:, w0:] += a2
        ds = ((wkeep[...] * stat[:, 0:1]) * (dprobs - stat[:, 128:129])).astype(BF16)
        dq = jnp.dot(ds, K, preferred_element_type=F32)
        for j, c in enumerate(columns(g)):
            dqj = dq[j * HALF:(j + 1) * HALF]
            dqb[0, rows, c] = dqj.astype(BF16)
            dqs = jnp.sum(dqj, axis=0, keepdims=True)
            if h == 0:
                sums[g, j:j + 1] = dqs
            else:
                sums[g, j:j + 1] += dqs
        a1 = jnp.dot(Q.T, ds, preferred_element_type=F32)
        if h == 0:
            dkt[:, :HWIN] = a1
            dkt[:, HWIN:] = jnp.zeros((HD, WIN - HWIN), F32)
        else:
            dkt[:, w0:] += a1

    def unit(g):
        w0 = HALF
        rows = slice(w0, w0 + HALF)
        K = kv[g, 0, w0:w0 + HWIN]
        V = kv[g, 1, w0:w0 + HWIN]
        Q = stacked(g, 1, q)
        D = stacked(g, 1, do)
        bias = jnp.concatenate([mask[rows, w0:w0 + HWIN]] * GROUP, 0)
        s = lax.dot_general(Q, K, NT, preferred_element_type=F32) * SCALE2 + bias
        dprobs = lax.dot_general(D, V, NT, preferred_element_type=F32)
        m = jnp.max(s, axis=1, keepdims=True)
        w = jnp.exp2(s - m)
        inv = 1.0 / jnp.sum(w, axis=1, keepdims=True)
        low = (w * inv).astype(BF16)
        o = jnp.dot(low, V, preferred_element_type=F32).astype(BF16)
        delta = jnp.sum(D.astype(F32) * o.astype(F32), axis=1, keepdims=True)
        ds = ((w * (inv * SCALE)) * (dprobs - delta)).astype(BF16)
        dvt[:, w0:] += jnp.dot(D.T, low, preferred_element_type=F32)
        dv = dvt[...].T
        part[g, 1] = dv
        sums[g, 6:7] = jnp.sum(dv, axis=0, keepdims=True)
        r1(g, 1)
        dq = jnp.dot(ds, K, preferred_element_type=F32)
        for j, c in enumerate(columns(g)):
            ob[0, rows, c] = o[j * HALF:(j + 1) * HALF]
            dqj = dq[j * HALF:(j + 1) * HALF]
            dqb[0, rows, c] = dqj.astype(BF16)
            sums[g, j:j + 1] += jnp.sum(dqj, axis=0, keepdims=True)
        dkt[:, w0:] += jnp.dot(Q.T, ds, preferred_element_type=F32)

    def finish(g):
        dk = dkt[...].T
        part[g, 0] = dk
        r1(g, 0)
        sums[g, 5:6] = jnp.sum(dk, axis=0, keepdims=True)
        sums[g, 7:8] = jnp.zeros((1, HD), F32)

    def both(step, g):
        step(g, 1)
        step(g, 0)

    def body(g, carry):
        complete(g)
        for c in qload(g):
            c.wait()
        unit_a(g, 0)

        @pl.when(g > 0)
        def _():
            both(r2, g - 1)

        @pl.when((g > 0) & (g < 3))
        def _():
            both(far, g + 1)

        unit_b(g, 0)

        @pl.when(g == 0)
        def _():
            both(far, 1)
            both(near, 2)
            for t in range(2):
                h1(3, t).start()

        @pl.when(g == 1)
        def _():
            both(near, 3)

        unit(g)

        @pl.when(g > 0)
        def _():
            both(r3, g - 1)

        @pl.when(g == 3)
        def _():
            r2(g, 1)

        finish(g)

        @pl.when(g > 1)
        def _():
            both(r4, g - 2)

        return carry

    lax.fori_loop(0, KVH, body, 0)

    b1[rank1] = sums[...]
    bias_send(b1, rank1, peer1, 8, 0, br1)
    r2(3, 0)
    r3(3, 1)
    total = bias_wait(b1, rank1, peer1, 8, 0, br1)
    b2[rank2] = total
    bias_send(b2, rank2, peer2, 4, 8, br2)
    r3(3, 0)
    total = bias_wait(b2, rank2, peer2, 4, 8, br2)
    b3[rank3] = total
    bias_send(b3, rank3, peer3, 8, 12, br3)
    both(r4, 2)
    both(r4, 3)
    total = bias_wait(b3, rank3, peer3, 8, 12, br3)
    for g in range(KVH):
        bias_out[g * GROUP:(g + 1) * GROUP] = total[g, 0:GROUP]
        bias_out[20 + g:21 + g] = total[g, 5:6]
        bias_out[24 + g:25 + g] = total[g, 6:7]

    def drain(g, carry):
        @pl.when(g > 0)
        def _():
            for t in range(2):
                h1(g, t).wait_send()

        for t in range(2):
            h2(g, t).wait_send()

        @pl.when(core == 0)
        def _():
            for t in range(2):
                l1(g, t).wait_send()
                l2_from0(g, t).wait_send()

        @pl.when(core == 1)
        def _():
            for t in range(2):
                l2_from1(g, t).wait_send()
                l3(g, t).wait_send()

        for t in range(2):
            ret(0, g, t, mate).wait_send()
            ret(1, g, t, mate).wait_send()
            ret(2, g, t, prv).wait_send()
            ret(3, g, t, prv).wait_send()
        return carry

    lax.fori_loop(0, KVH, drain, 0)


def on_device(queries, key_rows, value_rows, grad_out, doc_lengths):
    hbm = pl.BlockSpec(memory_space=pl.ANY)
    vmem = pl.BlockSpec(memory_space=pltpu.VMEM)
    dma = pltpu.SemaphoreType.DMA
    shapes = [((1, TOK, KVH * GW), BF16)] * 2 + [((1, TOK, KVH * HD), BF16)] * 2 + [((28, HD), F32)]
    held = pl.pallas_call(
        kernel,
        out_shape=[pltpu.VMEM(*a) for a in shapes],
        in_specs=[pl.BlockSpec(memory_space=pltpu.SMEM)] + [hbm] * 4,
        out_specs=[vmem] * 5,
        scratch_shapes=[
            pltpu.VMEM((TOK, KVH * GW), BF16),
            pltpu.VMEM((TOK, KVH * GW), BF16),
            pltpu.VMEM((KVH, 2, WIN, HD), BF16),
            pltpu.VMEM((KVH, 2, WIN, HD), F32),
            pltpu.VMEM((KVH, 4, 2, TOK, HD), BF16),
            pltpu.VMEM((KVH, 4, 2, TOK, HD), BF16),
            pltpu.VMEM((TOK, WIN), F32),
            pltpu.VMEM((HD, WIN), F32),
            pltpu.VMEM((HD, WIN), F32),
            pltpu.VMEM((GROUP * HALF, HWIN), F32),
            pltpu.VMEM((GROUP * HALF, HWIN), BF16),
            pltpu.VMEM((GROUP * HALF, 256), F32),
            pltpu.VMEM((KVH, 8, HD), F32),
            pltpu.VMEM((8, KVH, 8, HD), F32),
            pltpu.VMEM((4, KVH, 8, HD), F32),
            pltpu.VMEM((8, KVH, 8, HD), F32),
            dma((KVH, 2)),
            dma((KVH, 2)),
            dma((KVH, 5, 2)),
            dma((KVH, 5, 2)),
            dma((KVH, 4, 2)),
            dma((KVH, 4, 2)),
            dma((20,)),
            dma((8,)),
            dma((4,)),
            dma((8,)),
        ],
        compiler_params=pltpu.CompilerParams(
            collective_id=0, has_side_effects=True, vmem_limit_bytes=54 * 1024 * 1024
        ),
        cost_estimate=pl.CostEstimate(flops=10_000_000_000, bytes_accessed=8_000_000, transcendentals=6_000_000),
    )(doc_lengths, queries, key_rows, value_rows, grad_out)
    o, dq, dk, dv, bias = held
    return o, dq, dk, dv, bias.reshape(28 * HD)


def solution(mesh):
    spec = P("dp", "ctx", None)
    return jax.shard_map(
        on_device,
        mesh=mesh,
        in_specs=(spec, spec, spec, spec, P("dp", None)),
        out_specs=(spec, spec, spec, spec, P()),
        check_vma=False,
    )
```

```python
import math

import jax
import jax.numpy as jnp
from jax import lax
from jax.experimental import pallas as pl
from jax.experimental.pallas import tpu as pltpu
from jax.sharding import PartitionSpec as P

KVH = 4
HD = 128
GROUP = 5
TOK = 256
SPAN = 4
WIN = (SPAN + 1) * TOK
HALF = 128
HWIN = SPAN * TOK + HALF
GW = GROUP * HD
DOCS = 32
SCALE = 1.0 / math.sqrt(HD)
SCALE2 = SCALE * math.log2(math.e)
NT = (((1,), (1,)), ((), ()))
MESH = pl.DeviceIdType.MESH
F32 = jnp.float32
BF16 = jnp.bfloat16


def kernel(
    lens, q_hbm, k_hbm, v_hbm, do_hbm,
    ob, dqb, dk_out, dv_out, bias_out,
    q, do, kv, part, stage, got, mask, dkt, dvt, pkeep, lowkeep, stat,
    sums, b1, b2, b3,
    load_sem, kv_sem,
    fs, fr, rs, rr, bs, br1, br2, br3,
):
    dp = lax.axis_index("dp")
    me = lax.axis_index("ctx")
    n = 64
    core = lax.rem(me, 2)
    nxt = lax.rem(me + 2, n)
    prv = lax.rem(me + n - 2, n)
    mate = me + 1 - 2 * core
    rank1 = lax.rem(me, 8)
    rank2 = lax.rem(me // 8, 4)
    zlo = me // 32
    rank3 = dp * 2 + zlo

    def peer1(d):
        return (dp, me - rank1 + lax.rem(rank1 + d, 8))

    def peer2(d):
        return (dp, me + 8 * (lax.rem(rank2 + d, 4) - rank2))

    def peer3(d):
        r = lax.rem(rank3 + d, 8)
        return (r // 2, me + 32 * (lax.rem(r, 2) - zlo))

    def kvload(g):
        c = g * HD
        return (
            pltpu.make_async_copy(k_hbm.at[0, :, pl.ds(c, HD)], kv.at[g, 0, pl.ds(SPAN * TOK, TOK)], kv_sem.at[g, 0]),
            pltpu.make_async_copy(v_hbm.at[0, :, pl.ds(c, HD)], kv.at[g, 1, pl.ds(SPAN * TOK, TOK)], kv_sem.at[g, 1]),
        )

    def qload(g):
        c = pl.ds(pl.multiple_of(g * GW, 128), GW)
        return (
            pltpu.make_async_copy(q_hbm.at[0, :, c], q.at[:, c], load_sem.at[g, 0]),
            pltpu.make_async_copy(do_hbm.at[0, :, c], do.at[:, c], load_sem.at[g, 1]),
        )

    def fwd(kind, g, t, src_slot, dst_slot, to):
        return pltpu.make_async_remote_copy(
            src_ref=kv.at[g, t, pl.ds(src_slot * TOK, TOK)],
            dst_ref=kv.at[g, t, pl.ds(dst_slot * TOK, TOK)],
            send_sem=fs.at[g, kind, t],
            recv_sem=fr.at[g, kind, t],
            device_id=(dp, to),
            device_id_type=MESH,
        )

    def h1(g, t):
        return fwd(0, g, t, 4, 2, nxt)

    def h2(g, t):
        return fwd(1, g, t, 2, 0, nxt)

    def l1(g, t):
        return fwd(2, g, t, 4, 3, mate)

    def l2_from0(g, t):
        return fwd(3, g, t, 2, 1, mate)

    def l2_from1(g, t):
        return fwd(3, g, t, 2, 3, mate)

    def l3(g, t):
        return fwd(4, g, t, 0, 1, mate)

    def near(g, t):
        h1(g, t).wait_recv()
        h2(g, t).start()

        @pl.when(core == 0)
        def _():
            l2_from0(g, t).start()

        @pl.when(core == 1)
        def _():
            l2_from1(g, t).start()

    def far(g, t):
        h2(g, t).wait_recv()

        @pl.when(core == 1)
        def _():
            l3(g, t).start()

    def complete(g):
        @pl.when(core == 0)
        def _():
            for t in range(2):
                l2_from1(g, t).wait_recv()
                l3(g, t).wait_recv()

        @pl.when(core == 1)
        def _():
            for t in range(2):
                l1(g, t).wait_recv()
                l2_from0(g, t).wait_recv()

    def mate_send(g):
        @pl.when(core == 0)
        def _():
            for t in range(2):
                l1(g, t).start()

    def ret(kind, g, t, to):
        return pltpu.make_async_remote_copy(
            src_ref=stage.at[g, kind, t],
            dst_ref=got.at[g, kind, t],
            send_sem=rs.at[g, kind, t],
            recv_sem=rr.at[g, kind, t],
            device_id=(dp, to),
            device_id_type=MESH,
        )

    def r1(g, t):
        for kind, slot in ((0, 1), (1, 3)):
            stage[g, kind, t] = part[g, t, slot * TOK:(slot + 1) * TOK].astype(BF16)
            ret(kind, g, t, mate).start()

    def r2(g, t):
        ret(0, g, t, mate).wait_recv()

        @pl.when(core == 0)
        def _():
            stage[g, 2, t] = part[g, t, 0:TOK].astype(BF16)

        @pl.when(core == 1)
        def _():
            stage[g, 2, t] = (part[g, t, 0:TOK] + got[g, 0, t].astype(F32)).astype(BF16)

        ret(2, g, t, prv).start()
        ret(1, g, t, mate).wait_recv()

        @pl.when(core == 0)
        def _():
            part[g, t, 2 * TOK:3 * TOK] += got[g, 0, t].astype(F32)
            part[g, t, 4 * TOK:] += got[g, 1, t].astype(F32)

        @pl.when(core == 1)
        def _():
            part[g, t, 2 * TOK:3 * TOK] += got[g, 1, t].astype(F32)

    def r3(g, t):
        ret(2, g, t, prv).wait_recv()
        stage[g, 3, t] = (part[g, t, 2 * TOK:3 * TOK] + got[g, 2, t].astype(F32)).astype(BF16)
        ret(3, g, t, prv).start()

    def r4(g, t):
        ret(3, g, t, prv).wait_recv()
        c = pl.ds(pl.multiple_of(g * HD, 128), HD)
        (dk_out, dv_out)[t][0, :, c] = (part[g, t, 4 * TOK:] + got[g, 3, t].astype(F32)).astype(BF16)

    def bias_send(buf, rank, peer, size, sem_at, recv):
        for d in range(1, size):
            pltpu.make_async_remote_copy(
                src_ref=buf.at[rank],
                dst_ref=buf.at[rank],
                send_sem=bs.at[sem_at + d],
                recv_sem=recv.at[rank],
                device_id=peer(d),
                device_id_type=MESH,
            ).start()

    def bias_wait(buf, rank, peer, size, sem_at, recv):
        for d in range(1, size):
            other = lax.rem(rank + d, size)
            pltpu.make_async_remote_copy(
                src_ref=buf.at[rank],
                dst_ref=buf.at[other],
                send_sem=bs.at[sem_at + d],
                recv_sem=recv.at[other],
                device_id=peer(d),
                device_id_type=MESH,
            ).wait()
        total = buf[0]
        for r in range(1, size):
            total = total + buf[r]
        return total

    for g in range(KVH):
        for c in kvload(g):
            c.start()
    for g in range(KVH):
        for c in qload(g):
            c.start()

    barrier = pltpu.get_barrier_semaphore()
    peers = [(dp, nxt), (dp, prv)]
    peers += [peer1(d) for d in range(1, 8)]
    peers += [peer2(d) for d in range(1, 4)]
    peers += [peer3(d) for d in range(1, 8)]
    for p in peers:
        pl.semaphore_signal(barrier, inc=1, device_id=p, device_id_type=MESH)
    pl.semaphore_wait(barrier, len(peers))

    for t in range(2):
        kvload(0)[t].wait()
        h1(0, t).start()
    mate_send(0)
    for g in range(1, KVH):
        for c in kvload(g):
            c.wait()
        mate_send(g)
    for t in range(2):
        h1(0, t).wait_send()
        h1(1, t).start()

    where = me * TOK
    t_pos = lax.broadcasted_iota(jnp.int32, (TOK, 128), 0) + where
    first = jnp.zeros((TOK, 128), jnp.int32)
    bound = jnp.int32(0)
    for i in range(DOCS):
        bound = bound + lens[0, i]
        first = jnp.where(t_pos >= bound, bound, first)
    for c in range(WIN // 128):
        s_pos = lax.broadcasted_iota(jnp.int32, (TOK, 128), 1) + (where - SPAN * TOK + c * 128)
        mask[:, c * 128:(c + 1) * 128] = jnp.where((s_pos >= first) & (s_pos <= t_pos), 0.0, -1e30).astype(F32)

    for t in range(2):
        near(0, t)
    for t in range(2):
        near(1, t)
    for t in range(2):
        far(0, t)
    for t in range(2):
        h1(2, t).start()

    def stacked(g, h, of):
        rows = slice(h * HALF, (h + 1) * HALF)
        return jnp.concatenate([of[rows, c] for c in columns(g)], 0)

    def columns(g):
        return [pl.ds(pl.multiple_of(g * GW + j * HD, 128), HD) for j in range(GROUP)]

    def unit_a(g, h):
        w0 = h * HALF
        rows = slice(w0, w0 + HALF)
        K = kv[g, 0, w0:w0 + HWIN]
        V = kv[g, 1, w0:w0 + HWIN]
        Q = stacked(g, h, q)
        D = stacked(g, h, do)
        bias = jnp.concatenate([mask[rows, w0:w0 + HWIN]] * GROUP, 0)
        s = lax.dot_general(Q, K, NT, preferred_element_type=F32) * SCALE2 + bias
        m = jnp.max(s, axis=1, keepdims=True)
        w = jnp.exp2(s - m)
        inv = 1.0 / jnp.sum(w, axis=1, keepdims=True)
        p = w * inv
        low = p.astype(BF16)
        o = jnp.dot(low, V, preferred_element_type=F32).astype(BF16)
        delta = jnp.sum(D.astype(F32) * o.astype(F32), axis=1, keepdims=True)
        for j, c in enumerate(columns(g)):
            ob[0, rows, c] = o[j * HALF:(j + 1) * HALF]
        pkeep[...] = p
        lowkeep[...] = low
        stat[...] = jnp.broadcast_to(delta, (GROUP * HALF, 128))

    def unit_b(g, h):
        w0 = h * HALF
        rows = slice(w0, w0 + HALF)
        K = kv[g, 0, w0:w0 + HWIN]
        V = kv[g, 1, w0:w0 + HWIN]
        Q = stacked(g, h, q)
        D = stacked(g, h, do)
        dprobs = lax.dot_general(D, V, NT, preferred_element_type=F32)
        a2 = jnp.dot(D.T, lowkeep[...], preferred_element_type=F32)
        if h == 0:
            dvt[:, :HWIN] = a2
            dvt[:, HWIN:] = jnp.zeros((HD, WIN - HWIN), F32)
        else:
            dvt[:, w0:] += a2
        ds = ((pkeep[...] * SCALE) * (dprobs - stat[:, 0:1])).astype(BF16)
        dq = jnp.dot(ds, K, preferred_element_type=F32)
        for j, c in enumerate(columns(g)):
            dqj = dq[j * HALF:(j + 1) * HALF]
            dqb[0, rows, c] = dqj.astype(BF16)
            dqs = jnp.sum(dqj, axis=0, keepdims=True)
            if h == 0:
                sums[g, j:j + 1] = dqs
            else:
                sums[g, j:j + 1] += dqs
        a1 = jnp.dot(Q.T, ds, preferred_element_type=F32)
        if h == 0:
            dkt[:, :HWIN] = a1
            dkt[:, HWIN:] = jnp.zeros((HD, WIN - HWIN), F32)
        else:
            dkt[:, w0:] += a1

    def unit(g):
        w0 = HALF
        rows = slice(w0, w0 + HALF)
        K = kv[g, 0, w0:w0 + HWIN]
        V = kv[g, 1, w0:w0 + HWIN]
        Q = stacked(g, 1, q)
        D = stacked(g, 1, do)
        bias = jnp.concatenate([mask[rows, w0:w0 + HWIN]] * GROUP, 0)
        s = lax.dot_general(Q, K, NT, preferred_element_type=F32) * SCALE2 + bias
        m = jnp.max(s, axis=1, keepdims=True)
        w = jnp.exp2(s - m)
        inv = 1.0 / jnp.sum(w, axis=1, keepdims=True)
        p = w * inv
        low = p.astype(BF16)
        o = jnp.dot(low, V, preferred_element_type=F32).astype(BF16)
        dprobs = lax.dot_general(D, V, NT, preferred_element_type=F32)
        delta = jnp.sum(D.astype(F32) * o.astype(F32), axis=1, keepdims=True)
        ds = ((p * SCALE) * (dprobs - delta)).astype(BF16)
        dvt[:, w0:] += jnp.dot(D.T, low, preferred_element_type=F32)
        dv = dvt[...].T
        part[g, 1] = dv
        sums[g, 6:7] = jnp.sum(dv, axis=0, keepdims=True)
        r1(g, 1)
        dq = jnp.dot(ds, K, preferred_element_type=F32)
        for j, c in enumerate(columns(g)):
            ob[0, rows, c] = o[j * HALF:(j + 1) * HALF]
            dqj = dq[j * HALF:(j + 1) * HALF]
            dqb[0, rows, c] = dqj.astype(BF16)
            sums[g, j:j + 1] += jnp.sum(dqj, axis=0, keepdims=True)
        dkt[:, w0:] += jnp.dot(Q.T, ds, preferred_element_type=F32)

    def finish(g):
        dk = dkt[...].T
        part[g, 0] = dk
        r1(g, 0)
        sums[g, 5:6] = jnp.sum(dk, axis=0, keepdims=True)
        sums[g, 7:8] = jnp.zeros((1, HD), F32)

    def both(step, g):
        step(g, 1)
        step(g, 0)

    def body(g, carry):
        complete(g)
        for c in qload(g):
            c.wait()
        unit_a(g, 0)

        @pl.when(g > 0)
        def _():
            both(r2, g - 1)

        @pl.when((g > 0) & (g < 3))
        def _():
            both(far, g + 1)

        unit_b(g, 0)

        @pl.when(g == 0)
        def _():
            both(far, 1)
            both(near, 2)
            for t in range(2):
                h1(3, t).start()

        @pl.when(g == 1)
        def _():
            both(near, 3)

        unit(g)

        finish(g)

        @pl.when((g > 0) & (g < 3))
        def _():
            both(r3, g - 1)

        @pl.when(g == 2)
        def _():
            both(r4, g - 2)

        return carry

    lax.fori_loop(0, KVH, body, 0)

    b1[rank1] = sums[...]
    bias_send(b1, rank1, peer1, 8, 0, br1)
    both(r2, 3)
    both(r3, 2)
    total = bias_wait(b1, rank1, peer1, 8, 0, br1)
    b2[rank2] = total
    bias_send(b2, rank2, peer2, 4, 8, br2)
    both(r3, 3)
    total = bias_wait(b2, rank2, peer2, 4, 8, br2)
    b3[rank3] = total
    bias_send(b3, rank3, peer3, 8, 12, br3)
    both(r4, 1)
    both(r4, 2)
    both(r4, 3)
    total = bias_wait(b3, rank3, peer3, 8, 12, br3)
    for g in range(KVH):
        bias_out[g * GROUP:(g + 1) * GROUP] = total[g, 0:GROUP]
        bias_out[20 + g:21 + g] = total[g, 5:6]
        bias_out[24 + g:25 + g] = total[g, 6:7]

    def drain(g, carry):
        @pl.when(g > 0)
        def _():
            for t in range(2):
                h1(g, t).wait_send()

        for t in range(2):
            h2(g, t).wait_send()

        @pl.when(core == 0)
        def _():
            for t in range(2):
                l1(g, t).wait_send()
                l2_from0(g, t).wait_send()

        @pl.when(core == 1)
        def _():
            for t in range(2):
                l2_from1(g, t).wait_send()
                l3(g, t).wait_send()

        for t in range(2):
            ret(0, g, t, mate).wait_send()
            ret(1, g, t, mate).wait_send()
            ret(2, g, t, prv).wait_send()
            ret(3, g, t, prv).wait_send()
        return carry

    lax.fori_loop(0, KVH, drain, 0)


def on_device(queries, key_rows, value_rows, grad_out, doc_lengths):
    hbm = pl.BlockSpec(memory_space=pl.ANY)
    vmem = pl.BlockSpec(memory_space=pltpu.VMEM)
    dma = pltpu.SemaphoreType.DMA
    shapes = [((1, TOK, KVH * GW), BF16)] * 2 + [((1, TOK, KVH * HD), BF16)] * 2 + [((28, HD), F32)]
    held = pl.pallas_call(
        kernel,
        out_shape=[pltpu.VMEM(*a) for a in shapes],
        in_specs=[pl.BlockSpec(memory_space=pltpu.SMEM)] + [hbm] * 4,
        out_specs=[vmem] * 5,
        scratch_shapes=[
            pltpu.VMEM((TOK, KVH * GW), BF16),
            pltpu.VMEM((TOK, KVH * GW), BF16),
            pltpu.VMEM((KVH, 2, WIN, HD), BF16),
            pltpu.VMEM((KVH, 2, WIN, HD), F32),
            pltpu.VMEM((KVH, 4, 2, TOK, HD), BF16),
            pltpu.VMEM((KVH, 4, 2, TOK, HD), BF16),
            pltpu.VMEM((TOK, WIN), F32),
            pltpu.VMEM((HD, WIN), F32),
            pltpu.VMEM((HD, WIN), F32),
            pltpu.VMEM((GROUP * HALF, HWIN), F32),
            pltpu.VMEM((GROUP * HALF, HWIN), BF16),
            pltpu.VMEM((GROUP * HALF, 128), F32),
            pltpu.VMEM((KVH, 8, HD), F32),
            pltpu.VMEM((8, KVH, 8, HD), F32),
            pltpu.VMEM((4, KVH, 8, HD), F32),
            pltpu.VMEM((8, KVH, 8, HD), F32),
            dma((KVH, 2)),
            dma((KVH, 2)),
            dma((KVH, 5, 2)),
            dma((KVH, 5, 2)),
            dma((KVH, 4, 2)),
            dma((KVH, 4, 2)),
            dma((20,)),
            dma((8,)),
            dma((4,)),
            dma((8,)),
        ],
        compiler_params=pltpu.CompilerParams(
            collective_id=0, has_side_effects=True, vmem_limit_bytes=54 * 1024 * 1024
        ),
        cost_estimate=pl.CostEstimate(flops=10_000_000_000, bytes_accessed=8_000_000, transcendentals=6_000_000),
    )(doc_lengths, queries, key_rows, value_rows, grad_out)
    o, dq, dk, dv, bias = held
    return o, dq, dk, dv, bias.reshape(28 * HD)


def solution(mesh):
    spec = P("dp", "ctx", None)
    return jax.shard_map(
        on_device,
        mesh=mesh,
        in_specs=(spec, spec, spec, spec, P("dp", None)),
        out_specs=(spec, spec, spec, spec, P()),
        check_vma=False,
    )
```

```python
import math

import jax
import jax.numpy as jnp
from jax import lax
from jax.experimental import pallas as pl
from jax.experimental.pallas import tpu as pltpu
from jax.sharding import PartitionSpec as P

KVH = 4
HD = 128
GROUP = 5
TOK = 256
SPAN = 4
WIN = (SPAN + 1) * TOK
HALF = 128
HWIN = SPAN * TOK + HALF
GW = GROUP * HD
DOCS = 32
SCALE = 1.0 / math.sqrt(HD)
SCALE2 = SCALE * math.log2(math.e)
NT = (((1,), (1,)), ((), ()))
MESH = pl.DeviceIdType.MESH
F32 = jnp.float32
BF16 = jnp.bfloat16


def kernel(
    lens, q_hbm, k_hbm, v_hbm, do_hbm,
    ob, dqb, dk_out, dv_out, bias_out,
    q, do, kv, part, stage, got, mask, dkt, dvt, pkeep, lowkeep, stat,
    sums, b1, b2, b3,
    load_sem, kv_sem,
    fs, fr, rs, rr, bs, br1, br2, br3,
):
    dp = lax.axis_index("dp")
    me = lax.axis_index("ctx")
    n = 64
    core = lax.rem(me, 2)
    nxt = lax.rem(me + 2, n)
    prv = lax.rem(me + n - 2, n)
    mate = me + 1 - 2 * core
    rank1 = lax.rem(me, 8)
    rank2 = lax.rem(me // 8, 4)
    zlo = me // 32
    rank3 = dp * 2 + zlo

    def peer1(d):
        return (dp, me - rank1 + lax.rem(rank1 + d, 8))

    def peer2(d):
        return (dp, me + 8 * (lax.rem(rank2 + d, 4) - rank2))

    def peer3(d):
        r = lax.rem(rank3 + d, 8)
        return (r // 2, me + 32 * (lax.rem(r, 2) - zlo))

    def kvload(g):
        c = g * HD
        return (
            pltpu.make_async_copy(k_hbm.at[0, :, pl.ds(c, HD)], kv.at[g, 0, pl.ds(SPAN * TOK, TOK)], kv_sem.at[g, 0]),
            pltpu.make_async_copy(v_hbm.at[0, :, pl.ds(c, HD)], kv.at[g, 1, pl.ds(SPAN * TOK, TOK)], kv_sem.at[g, 1]),
        )

    def qload(g):
        c = pl.ds(pl.multiple_of(g * GW, 128), GW)
        return (
            pltpu.make_async_copy(q_hbm.at[0, :, c], q.at[:, c], load_sem.at[g, 0]),
            pltpu.make_async_copy(do_hbm.at[0, :, c], do.at[:, c], load_sem.at[g, 1]),
        )

    def fwd(kind, g, t, src_slot, dst_slot, to):
        return pltpu.make_async_remote_copy(
            src_ref=kv.at[g, t, pl.ds(src_slot * TOK, TOK)],
            dst_ref=kv.at[g, t, pl.ds(dst_slot * TOK, TOK)],
            send_sem=fs.at[g, kind, t],
            recv_sem=fr.at[g, kind, t],
            device_id=(dp, to),
            device_id_type=MESH,
        )

    def h1(g, t):
        return fwd(0, g, t, 4, 2, nxt)

    def h2(g, t):
        return fwd(1, g, t, 2, 0, nxt)

    def l1(g, t):
        return fwd(2, g, t, 4, 3, mate)

    def l2_from0(g, t):
        return fwd(3, g, t, 2, 1, mate)

    def l2_from1(g, t):
        return fwd(3, g, t, 2, 3, mate)

    def l3(g, t):
        return fwd(4, g, t, 0, 1, mate)

    def near(g, t):
        h1(g, t).wait_recv()
        h2(g, t).start()

        @pl.when(core == 0)
        def _():
            l2_from0(g, t).start()

        @pl.when(core == 1)
        def _():
            l2_from1(g, t).start()

    def far(g, t):
        h2(g, t).wait_recv()

        @pl.when(core == 1)
        def _():
            l3(g, t).start()

    def complete(g):
        @pl.when(core == 0)
        def _():
            for t in range(2):
                l2_from1(g, t).wait_recv()
                l3(g, t).wait_recv()

        @pl.when(core == 1)
        def _():
            for t in range(2):
                l1(g, t).wait_recv()
                l2_from0(g, t).wait_recv()

    def mate_send(g):
        @pl.when(core == 0)
        def _():
            for t in range(2):
                l1(g, t).start()

    def ret(kind, g, t, to):
        return pltpu.make_async_remote_copy(
            src_ref=stage.at[g, kind, t],
            dst_ref=got.at[g, kind, t],
            send_sem=rs.at[g, kind, t],
            recv_sem=rr.at[g, kind, t],
            device_id=(dp, to),
            device_id_type=MESH,
        )

    def r1(g, t):
        for kind, slot in ((0, 1), (1, 3)):
            stage[g, kind, t] = part[g, t, slot * TOK:(slot + 1) * TOK].astype(BF16)
            ret(kind, g, t, mate).start()

    def r2(g, t):
        ret(0, g, t, mate).wait_recv()

        @pl.when(core == 0)
        def _():
            stage[g, 2, t] = part[g, t, 0:TOK].astype(BF16)

        @pl.when(core == 1)
        def _():
            stage[g, 2, t] = (part[g, t, 0:TOK] + got[g, 0, t].astype(F32)).astype(BF16)

        ret(2, g, t, prv).start()
        ret(1, g, t, mate).wait_recv()

        @pl.when(core == 0)
        def _():
            part[g, t, 2 * TOK:3 * TOK] += got[g, 0, t].astype(F32)
            part[g, t, 4 * TOK:] += got[g, 1, t].astype(F32)

        @pl.when(core == 1)
        def _():
            part[g, t, 2 * TOK:3 * TOK] += got[g, 1, t].astype(F32)

    def r3(g, t):
        ret(2, g, t, prv).wait_recv()
        stage[g, 3, t] = (part[g, t, 2 * TOK:3 * TOK] + got[g, 2, t].astype(F32)).astype(BF16)
        ret(3, g, t, prv).start()

    def r4(g, t):
        ret(3, g, t, prv).wait_recv()
        c = pl.ds(pl.multiple_of(g * HD, 128), HD)
        (dk_out, dv_out)[t][0, :, c] = (part[g, t, 4 * TOK:] + got[g, 3, t].astype(F32)).astype(BF16)

    def bias_send(buf, rank, peer, size, sem_at, recv):
        for d in range(1, size):
            pltpu.make_async_remote_copy(
                src_ref=buf.at[rank],
                dst_ref=buf.at[rank],
                send_sem=bs.at[sem_at + d],
                recv_sem=recv.at[rank],
                device_id=peer(d),
                device_id_type=MESH,
            ).start()

    def bias_wait(buf, rank, peer, size, sem_at, recv):
        for d in range(1, size):
            other = lax.rem(rank + d, size)
            pltpu.make_async_remote_copy(
                src_ref=buf.at[rank],
                dst_ref=buf.at[other],
                send_sem=bs.at[sem_at + d],
                recv_sem=recv.at[other],
                device_id=peer(d),
                device_id_type=MESH,
            ).wait()
        total = buf[0]
        for r in range(1, size):
            total = total + buf[r]
        return total

    for g in range(KVH):
        for c in kvload(g):
            c.start()
    for g in range(KVH):
        for c in qload(g):
            c.start()

    barrier = pltpu.get_barrier_semaphore()
    peers = [(dp, nxt), (dp, prv)]
    peers += [peer1(d) for d in range(1, 8)]
    peers += [peer2(d) for d in range(1, 4)]
    peers += [peer3(d) for d in range(1, 8)]
    for p in peers:
        pl.semaphore_signal(barrier, inc=1, device_id=p, device_id_type=MESH)
    pl.semaphore_wait(barrier, len(peers))

    for t in range(2):
        kvload(0)[t].wait()
        h1(0, t).start()
    mate_send(0)
    for g in range(1, KVH):
        for c in kvload(g):
            c.wait()
        mate_send(g)
    for t in range(2):
        h1(0, t).wait_send()
        h1(1, t).start()

    where = me * TOK
    t_pos = lax.broadcasted_iota(jnp.int32, (TOK, 128), 0) + where
    first = jnp.zeros((TOK, 128), jnp.int32)
    bound = jnp.int32(0)
    for i in range(DOCS):
        bound = bound + lens[0, i]
        first = jnp.where(t_pos >= bound, bound, first)
    for c in range(WIN // 128):
        s_pos = lax.broadcasted_iota(jnp.int32, (TOK, 128), 1) + (where - SPAN * TOK + c * 128)
        mask[:, c * 128:(c + 1) * 128] = jnp.where((s_pos >= first) & (s_pos <= t_pos), 0.0, -1e30).astype(F32)

    for t in range(2):
        near(0, t)
    for t in range(2):
        near(1, t)
    for t in range(2):
        far(0, t)
    for t in range(2):
        h1(2, t).start()

    def stacked(g, h, of):
        rows = slice(h * HALF, (h + 1) * HALF)
        return jnp.concatenate([of[rows, c] for c in columns(g)], 0)

    def columns(g):
        return [pl.ds(pl.multiple_of(g * GW + j * HD, 128), HD) for j in range(GROUP)]

    def unit_a(g, h):
        w0 = h * HALF
        rows = slice(w0, w0 + HALF)
        K = kv[g, 0, w0:w0 + HWIN]
        V = kv[g, 1, w0:w0 + HWIN]
        Q = stacked(g, h, q)
        D = stacked(g, h, do)
        bias = jnp.concatenate([mask[rows, w0:w0 + HWIN]] * GROUP, 0)
        s = lax.dot_general(Q, K, NT, preferred_element_type=F32) * SCALE2 + bias
        m = jnp.max(s, axis=1, keepdims=True)
        w = jnp.exp2(s - m)
        inv = 1.0 / jnp.sum(w, axis=1, keepdims=True)
        p = w * inv
        low = p.astype(BF16)
        o = jnp.dot(low, V, preferred_element_type=F32).astype(BF16)
        delta = jnp.sum(D.astype(F32) * o.astype(F32), axis=1, keepdims=True)
        for j, c in enumerate(columns(g)):
            ob[0, rows, c] = o[j * HALF:(j + 1) * HALF]
        pkeep[...] = p
        lowkeep[...] = low
        stat[...] = jnp.broadcast_to(delta, (GROUP * HALF, 128))

    def unit_b(g, h):
        w0 = h * HALF
        rows = slice(w0, w0 + HALF)
        K = kv[g, 0, w0:w0 + HWIN]
        V = kv[g, 1, w0:w0 + HWIN]
        Q = stacked(g, h, q)
        D = stacked(g, h, do)
        dprobs = lax.dot_general(D, V, NT, preferred_element_type=F32)
        a2 = jnp.dot(D.T, lowkeep[...], preferred_element_type=F32)
        if h == 0:
            dvt[:, :HWIN] = a2
            dvt[:, HWIN:] = jnp.zeros((HD, WIN - HWIN), F32)
        else:
            dvt[:, w0:] += a2
        ds = ((pkeep[...] * SCALE) * (dprobs - stat[:, 0:1])).astype(BF16)
        dq = jnp.dot(ds, K, preferred_element_type=F32)
        for j, c in enumerate(columns(g)):
            dqj = dq[j * HALF:(j + 1) * HALF]
            dqb[0, rows, c] = dqj.astype(BF16)
            dqs = jnp.sum(dqj, axis=0, keepdims=True)
            if h == 0:
                sums[g, j:j + 1] = dqs
            else:
                sums[g, j:j + 1] += dqs
        a1 = jnp.dot(Q.T, ds, preferred_element_type=F32)
        if h == 0:
            dkt[:, :HWIN] = a1
            dkt[:, HWIN:] = jnp.zeros((HD, WIN - HWIN), F32)
        else:
            dkt[:, w0:] += a1

    def unit(g):
        w0 = HALF
        rows = slice(w0, w0 + HALF)
        K = kv[g, 0, w0:w0 + HWIN]
        V = kv[g, 1, w0:w0 + HWIN]
        Q = stacked(g, 1, q)
        D = stacked(g, 1, do)
        bias = jnp.concatenate([mask[rows, w0:w0 + HWIN]] * GROUP, 0)
        s = lax.dot_general(Q, K, NT, preferred_element_type=F32) * SCALE2 + bias
        m = jnp.max(s, axis=1, keepdims=True)
        w = jnp.exp2(s - m)
        inv = 1.0 / jnp.sum(w, axis=1, keepdims=True)
        p = w * inv
        low = p.astype(BF16)
        o = jnp.dot(low, V, preferred_element_type=F32).astype(BF16)
        dprobs = lax.dot_general(D, V, NT, preferred_element_type=F32)
        delta = jnp.sum(D.astype(F32) * o.astype(F32), axis=1, keepdims=True)
        ds = ((p * SCALE) * (dprobs - delta)).astype(BF16)
        dvt[:, w0:] += jnp.dot(D.T, low, preferred_element_type=F32)
        dv = dvt[...].T
        part[g, 1] = dv
        sums[g, 6:7] = jnp.sum(dv, axis=0, keepdims=True)
        r1(g, 1)
        dq = jnp.dot(ds, K, preferred_element_type=F32)
        for j, c in enumerate(columns(g)):
            ob[0, rows, c] = o[j * HALF:(j + 1) * HALF]
            dqj = dq[j * HALF:(j + 1) * HALF]
            dqb[0, rows, c] = dqj.astype(BF16)
            sums[g, j:j + 1] += jnp.sum(dqj, axis=0, keepdims=True)
        dkt[:, w0:] += jnp.dot(Q.T, ds, preferred_element_type=F32)

    def finish(g):
        dk = dkt[...].T
        part[g, 0] = dk
        sums[g, 5:6] = jnp.sum(dk, axis=0, keepdims=True)
        sums[g, 7:8] = jnp.zeros((1, HD), F32)

        @pl.when(g == 3)
        def _():
            b1[rank1] = sums[...]
            bias_send(b1, rank1, peer1, 8, 0, br1)

        r1(g, 0)

    def both(step, g):
        step(g, 1)
        step(g, 0)

    def body(g, carry):
        complete(g)
        for c in qload(g):
            c.wait()
        unit_a(g, 0)

        @pl.when(g > 0)
        def _():
            both(r2, g - 1)

        @pl.when((g > 0) & (g < 3))
        def _():
            both(far, g + 1)

        unit_b(g, 0)

        @pl.when(g == 0)
        def _():
            both(far, 1)
            both(near, 2)
            for t in range(2):
                h1(3, t).start()

        @pl.when(g == 1)
        def _():
            both(near, 3)

        unit(g)

        finish(g)

        @pl.when((g > 0) & (g < 3))
        def _():
            both(r3, g - 1)

        @pl.when(g == 2)
        def _():
            both(r4, g - 2)

        return carry

    lax.fori_loop(0, KVH, body, 0)

    both(r2, 3)
    both(r3, 2)
    total = bias_wait(b1, rank1, peer1, 8, 0, br1)
    b2[rank2] = total
    bias_send(b2, rank2, peer2, 4, 8, br2)
    both(r3, 3)
    total = bias_wait(b2, rank2, peer2, 4, 8, br2)
    b3[rank3] = total
    bias_send(b3, rank3, peer3, 8, 12, br3)
    both(r4, 1)
    both(r4, 2)
    both(r4, 3)
    total = bias_wait(b3, rank3, peer3, 8, 12, br3)
    for g in range(KVH):
        bias_out[g * GROUP:(g + 1) * GROUP] = total[g, 0:GROUP]
        bias_out[20 + g:21 + g] = total[g, 5:6]
        bias_out[24 + g:25 + g] = total[g, 6:7]

    def drain(g, carry):
        @pl.when(g > 0)
        def _():
            for t in range(2):
                h1(g, t).wait_send()

        for t in range(2):
            h2(g, t).wait_send()

        @pl.when(core == 0)
        def _():
            for t in range(2):
                l1(g, t).wait_send()
                l2_from0(g, t).wait_send()

        @pl.when(core == 1)
        def _():
            for t in range(2):
                l2_from1(g, t).wait_send()
                l3(g, t).wait_send()

        for t in range(2):
            ret(0, g, t, mate).wait_send()
            ret(1, g, t, mate).wait_send()
            ret(2, g, t, prv).wait_send()
            ret(3, g, t, prv).wait_send()
        return carry

    lax.fori_loop(0, KVH, drain, 0)


def on_device(queries, key_rows, value_rows, grad_out, doc_lengths):
    hbm = pl.BlockSpec(memory_space=pl.ANY)
    vmem = pl.BlockSpec(memory_space=pltpu.VMEM)
    dma = pltpu.SemaphoreType.DMA
    shapes = [((1, TOK, KVH * GW), BF16)] * 2 + [((1, TOK, KVH * HD), BF16)] * 2 + [((28, HD), F32)]
    held = pl.pallas_call(
        kernel,
        out_shape=[pltpu.VMEM(*a) for a in shapes],
        in_specs=[pl.BlockSpec(memory_space=pltpu.SMEM)] + [hbm] * 4,
        out_specs=[vmem] * 5,
        scratch_shapes=[
            pltpu.VMEM((TOK, KVH * GW), BF16),
            pltpu.VMEM((TOK, KVH * GW), BF16),
            pltpu.VMEM((KVH, 2, WIN, HD), BF16),
            pltpu.VMEM((KVH, 2, WIN, HD), F32),
            pltpu.VMEM((KVH, 4, 2, TOK, HD), BF16),
            pltpu.VMEM((KVH, 4, 2, TOK, HD), BF16),
            pltpu.VMEM((TOK, WIN), F32),
            pltpu.VMEM((HD, WIN), F32),
            pltpu.VMEM((HD, WIN), F32),
            pltpu.VMEM((GROUP * HALF, HWIN), F32),
            pltpu.VMEM((GROUP * HALF, HWIN), BF16),
            pltpu.VMEM((GROUP * HALF, 128), F32),
            pltpu.VMEM((KVH, 8, HD), F32),
            pltpu.VMEM((8, KVH, 8, HD), F32),
            pltpu.VMEM((4, KVH, 8, HD), F32),
            pltpu.VMEM((8, KVH, 8, HD), F32),
            dma((KVH, 2)),
            dma((KVH, 2)),
            dma((KVH, 5, 2)),
            dma((KVH, 5, 2)),
            dma((KVH, 4, 2)),
            dma((KVH, 4, 2)),
            dma((20,)),
            dma((8,)),
            dma((4,)),
            dma((8,)),
        ],
        compiler_params=pltpu.CompilerParams(
            collective_id=0, has_side_effects=True, vmem_limit_bytes=54 * 1024 * 1024
        ),
        cost_estimate=pl.CostEstimate(flops=10_000_000_000, bytes_accessed=8_000_000, transcendentals=6_000_000),
    )(doc_lengths, queries, key_rows, value_rows, grad_out)
    o, dq, dk, dv, bias = held
    return o, dq, dk, dv, bias.reshape(28 * HD)


def solution(mesh):
    spec = P("dp", "ctx", None)
    return jax.shard_map(
        on_device,
        mesh=mesh,
        in_specs=(spec, spec, spec, spec, P("dp", None)),
        out_specs=(spec, spec, spec, spec, P()),
        check_vma=False,
    )
```
